128 devices in a mesh: dp: 16 (over y_lo, x, core), tensor: 8 (over z, y_hi).
Axes of the slice: x: 4, y: 4 (y_hi: 2, y_lo: 2; y = y_hi * 2 + y_lo), z: 4, core: 2. Of those that a mesh axis runs over, the one named last changes fastest.
Arguments:
- tokens: bfloat16 [8192, 3200], P('dp', 'tensor'), may hold values from -6 to 6
- vit_gain: float32 [3200], replicated, may hold values from 0.1 to 1.9
- fc_up: bfloat16 [3200, 12800], P('dp', 'tensor'), may hold values from -0.109375 to 0.109375
- fc_down: bfloat16 [3200, 12800], P('dp', 'tensor'), may hold values from -0.0546875 to 0.0546875
- layer_scale: float32 [3200], replicated, may hold values from 0.3 to 1
- proj_gain: float32 [12800], replicated, may hold values from 0.1 to 1.9
- proj_bias: float32 [12800], replicated, may hold values from -3 to 3
- proj_in: bfloat16 [12800, 8192], P('dp', 'tensor'), may hold values from -0.0546875 to 0.0546875
- proj_out: bfloat16 [8192, 8192], P('tensor'), may hold values from -0.0625 to 0.0625
- clip_frames: int32 [1], replicated, may hold values from 64 to 128
- slot_perm: int32 [128], replicated, may hold values from 0 to 127, as said below
Outputs:
- embedded: bfloat16 [2048, 8192], P('dp', 'tensor')
The draws below stay inside these ranges and needn't reach their ends.
Inputs may be any that keep to these rules, and one draw needn't show every extreme that they name: slot_perm is a permutation; two frames f != g with f // 8 == g // 8 never have slot_perm[f] // 8 == slot_perm[g] // 8.
All inputs are finite; a program needn't handle non-finite values.
Results may differ from the reference program's by a relative error of at most 0.022.
Values may be sent and summed in bfloat16 or wider, within the bound.
No kernel may reach another device: no remote copies, remote signals or barrier semaphores. Data moves between devices by JAX's collectives and lax.ppermute only.
A program may use at most 128 MiB of HBM per device.

```python
import math
import jax
import jax.numpy as jnp
from jax import lax

D = 3200
FF = 12800
P_SIZE = 8192
S = 16
FR_DEV = 8
FRAMES = 128


def draw_slot_perm(key, part):
    key = jax.random.fold_in(key, 7)
    key_base, key_offset, key_place = jax.random.split(key, 3)
    groups = FRAMES // FR_DEV
    base = jax.random.permutation(key_base, groups)
    offsets = jax.random.permutation(key_offset, groups)[:FR_DEV]
    target = (base[:, None] + offsets[None, :]) % groups
    places = jax.vmap(lambda k: jax.random.permutation(k, FR_DEV))(jax.random.split(key_place, groups))
    column = jnp.broadcast_to(jnp.arange(FR_DEV)[None, :], (groups, FR_DEV))
    inside = places[target, column]
    return (target * FR_DEV + inside).reshape(FRAMES).astype(jnp.int32)


def shard_levels(stream_key, shape, shards, low, largest):
    level = 1.0
    for dim, parts in shards:
        steps = jax.random.uniform(jax.random.fold_in(jax.random.fold_in(stream_key, 6), dim), (parts,), jnp.float32, low / len(shards), largest / len(shards))
        level = level * jnp.repeat(jnp.exp(steps), shape[dim] // parts).reshape((-1,) + (1,) * (len(shape) - 1 - dim))
    return level


def scatter_about(stream_key, shape, width, reach, cuts=(), held_as=jnp.bfloat16):
    drawn = jax.random.normal(stream_key, shape, jnp.float32) * width
    if len(cuts) > 0:
        drawn = shard_levels(stream_key, shape, cuts, -0.22, 0.18) * drawn
    return jnp.clip(drawn, min=-reach, max=reach).astype(held_as)


def setup_inputs(seed: int = 0) -> dict:
    keys = jax.random.split(jax.random.key(seed), 12)
    tokens = scatter_about(keys[0], (FRAMES * 4 * S, D), 1.0, 6.0, ((0, 16), (1, 8)))
    vit_gain = jnp.clip(1.0 + 0.18 * jax.random.normal(keys[1], (D,), jnp.float32), 0.1, 1.9)
    fc_up = scatter_about(keys[2], (D, FF), D ** -0.5, 0.109375, ((0, 16), (1, 8)))
    fc_down = scatter_about(keys[3], (D, FF), FF ** -0.5, 0.0546875, ((0, 16), (1, 8)))
    layer_scale = jnp.clip(jnp.exp(jax.random.uniform(keys[4], (D,), jnp.float32, math.log(0.3), math.log(1.0))), 0.3, 1.0)
    proj_gain = jnp.clip(1.0 + 0.18 * jax.random.normal(keys[5], (4 * D,), jnp.float32), 0.1, 1.9)
    proj_bias = scatter_about(keys[6], (4 * D,), 0.5, 3.0, (), jnp.float32)
    proj_in = scatter_about(keys[7], (4 * D, P_SIZE), (4 * D) ** -0.5, 0.0546875, ((0, 16), (1, 8)))
    proj_out = scatter_about(keys[8], (P_SIZE, P_SIZE), P_SIZE ** -0.5, 0.0625, ((0, 8),))
    clip_frames = jax.random.randint(keys[9], (1,), FRAMES // 2, FRAMES + 1).astype(jnp.int32)
    slot_perm = draw_slot_perm(jax.random.fold_in(keys[11], 71), 0)
    return dict(tokens=tokens, vit_gain=vit_gain, fc_up=fc_up, fc_down=fc_down, layer_scale=layer_scale, proj_gain=proj_gain, proj_bias=proj_bias, proj_in=proj_in, proj_out=proj_out, clip_frames=clip_frames, slot_perm=slot_perm)


def reference(tokens, vit_gain, fc_up, fc_down, layer_scale, proj_gain, proj_bias, proj_in, proj_out, clip_frames, slot_perm):
    xf = tokens.astype(jnp.float32)
    normed = (xf * lax.rsqrt(lax.optimization_barrier(jnp.mean(xf * xf, axis=-1, keepdims=True)) + 1e-06) * vit_gain).astype(jnp.bfloat16)
    act = jnp.dot(normed, fc_up, preferred_element_type=jnp.float32)
    hidden = jax.nn.gelu(act, approximate=False).astype(jnp.bfloat16)
    branch = lax.dot_general(hidden, fc_down, (((1,), (1,)), ((), ())), preferred_element_type=jnp.float32)
    vision_out = (xf + layer_scale * branch).astype(jnp.bfloat16)
    merged = vision_out.reshape(-1, 4 * D).astype(jnp.float32)
    mean = lax.optimization_barrier(jnp.mean(merged, axis=-1, keepdims=True))
    centred = merged - mean
    var = lax.optimization_barrier(jnp.mean(centred * centred, axis=-1, keepdims=True))
    shuffled = (centred * lax.rsqrt(var + 1e-05) * proj_gain + proj_bias).astype(jnp.bfloat16)
    pre = jnp.dot(shuffled, proj_in, preferred_element_type=jnp.float32)
    projected = jax.nn.gelu(pre, approximate=False).astype(jnp.bfloat16)
    frames = projected.reshape(FRAMES, S, P_SIZE)
    valid = jnp.arange(FRAMES, dtype=jnp.int32) < clip_frames[0]
    frames = jnp.where(valid[:, None, None], frames, jnp.zeros_like(frames))
    slots = jnp.zeros_like(frames).at[slot_perm].set(frames).reshape(FRAMES * S, P_SIZE)
    return jnp.dot(slots, proj_out, preferred_element_type=jnp.float32).astype(jnp.bfloat16)
```

```python
import jax
import jax.numpy as jnp
from jax import lax
from jax.experimental import pallas as pl
from jax.experimental.pallas import tpu as pltpu
from jax.sharding import PartitionSpec as P

AXES = ("dp", "tensor")
BF = jnp.bfloat16
F32 = jnp.float32


def hop(move):
    pairs = []
    for yl in range(2):
        for x in range(4):
            for c in range(2):
                for z in range(4):
                    for yh in range(2):
                        x2, yl2, c2, z2, yh2 = move(x, yl, c, z, yh)
                        src = ((yl * 4 + x) * 2 + c) * 8 + z * 2 + yh
                        dst = ((yl2 * 4 + x2 % 4) * 2 + c2) * 8 + (z2 % 4) * 2 + yh2
                        pairs.append((src, dst))
    return pairs


CORE = hop(lambda x, yl, c, z, yh: (x, yl, 1 - c, z, yh))
YLO = hop(lambda x, yl, c, z, yh: (x, 1 - yl, c, z, yh))
YHI = hop(lambda x, yl, c, z, yh: (x, yl, c, z, 1 - yh))
XP = hop(lambda x, yl, c, z, yh: (x + 1, yl, c, z, yh))
XM = hop(lambda x, yl, c, z, yh: (x + 3, yl, c, z, yh))
ZP = hop(lambda x, yl, c, z, yh: (x, yl, c, z + 1, yh))
ZM = hop(lambda x, yl, c, z, yh: (x, yl, c, z + 3, yh))
XBOTH = hop(lambda x, yl, c, z, yh: (x + 1 + 2 * c, yl, c, z, yh))
ZBOTH = hop(lambda x, yl, c, z, yh: (x, yl, c, z + 1 + 2 * c, yh))


def go(a, pairs):
    return lax.ppermute(a, AXES, pairs)


def flip(a, d):
    return a + d - 2 * a * d


def coords():
    dp = lax.axis_index("dp")
    te = lax.axis_index("tensor")
    return (dp // 2) % 4, dp // 8, dp % 2, te // 2, te % 2


SHARDS = (
    (0, 0, 0),
    (0, 0, 1),
    (0, 1, 0),
    (0, 1, 1),
    (1, 0, 0),
    (-1, 0, 1),
    (1, 0, 1),
    (-1, 0, 0),
    (2, 0, 0),
    (2, 0, 1),
    (1, 1, 0),
    (-1, 1, 1),
    (1, 1, 1),
    (-1, 1, 0),
    (2, 1, 0),
    (2, 1, 1),
)
FIRST = 10


def shard_place(k):
    x, yl, c, _, _ = coords()
    step, dy, dc = SHARDS[k]
    if step == 2:
        dx = 2
    else:
        dx = step * (2 * c - 1) + 4
    return (flip(yl, dy) * 4 + (x + dx) % 4) * 2 + flip(c, dc)


def phase(*values):
    return lax.optimization_barrier(values)


def gather_tensor(a):
    zm_o, zp_o, p = phase(go(a, ZP), go(a, ZM), go(a, YHI))
    half = a.shape[0] // 2
    zm_p, zp_p = go(p, ZP), go(p, ZM)
    z2_o = jnp.concatenate([go(zm_o[:half], ZP), go(zp_o[half:], ZM)], axis=0)
    z2_p = go(z2_o, YHI)
    return [a, p, zp_o, zp_p, z2_o, z2_p, zm_o, zm_p]


def add(a, b):
    return a.astype(F32) + b.astype(F32)


def ring_sum(u, plus, minus):
    half = u[2].shape[0] // 2
    up = go(u[2][:half], plus)
    down = go(u[2][half:], minus)
    first = jnp.concatenate([add(u[1][:half], up).astype(BF), u[1][half:]], axis=0)
    third = jnp.concatenate([u[3][:half], add(u[3][half:], down).astype(BF)], axis=0)
    got_up = go(first, plus)
    got_down = go(third, minus)
    return u[0].astype(F32) + got_up.astype(F32) + got_down.astype(F32)


def gelu(v):
    return 0.5 * v * (1.0 + lax.erf(v * 0.7071067811865476))


ANY = pl.BlockSpec(memory_space=pl.ANY)
VMEM = pl.BlockSpec(memory_space=pltpu.VMEM)
SMEM = pl.BlockSpec(memory_space=pltpu.SMEM)


def frame_of(r):
    _, _, _, z, yh = coords()
    return ((z + r // 2) % 4) * 2 + flip(yh, r % 2)


def up_body(place, *refs):
    blocks, gain, shards = refs[:8], refs[8], refs[9:25]
    out, res, xs, held, acc, squares, xsems, sems = refs[25:]
    xcopies = [
        pltpu.make_async_copy(blocks[i], xs.at[pl.ds(frame_of(i) * 2, 2)], xsems.at[i]) for i in range(8)
    ]
    copies = [pltpu.make_async_copy(shards[k], held.at[k], sems.at[k]) for k in range(16)]
    for cp in xcopies + copies:
        cp.start()
    acc[...] = jnp.zeros_like(acc)
    squares[...] = jnp.zeros_like(squares)
    for cp in xcopies:
        cp.wait()

    def shard(k, _):
        pltpu.make_async_copy(shards[0], held.at[k], sems.at[k]).wait()
        p = place[k]
        v = xs[p].astype(F32)
        squares[...] += v * v
        acc[...] += jnp.dot((v * gain[p]).astype(BF), held[k], preferred_element_type=F32)
        return 0

    lax.fori_loop(0, 16, shard, 0)

    def finish(r, _):
        at = pl.ds(pl.multiple_of(frame_of(r) * 64, 64), 64)
        scale = lax.rsqrt(jnp.sum(squares[at, :], axis=1, keepdims=True) * (1.0 / 3200.0) + 1e-06)
        out[pl.ds(pl.multiple_of(r * 64, 64), 64), :] = gelu(acc[at, :] * scale).astype(BF)
        return 0

    lax.fori_loop(0, 8, finish, 0)
    own = pl.ds(pl.multiple_of(frame_of(0) * 64, 64), 64)
    for p in range(16):
        res[p] = xs[p, own, :]


def up(place, blocks, gain, shards):
    return pl.pallas_call(
        up_body,
        out_shape=(jax.ShapeDtypeStruct((512, 1600), BF), jax.ShapeDtypeStruct((16, 64, 200), BF)),
        in_specs=[SMEM] + [ANY] * 8 + [VMEM] + [ANY] * 16,
        out_specs=(VMEM, VMEM),
        scratch_shapes=[
            pltpu.VMEM((16, 512, 200), BF),
            pltpu.VMEM((16, 200, 1600), BF),
            pltpu.VMEM((512, 1600), F32),
            pltpu.VMEM((512, 200), F32),
            pltpu.SemaphoreType.DMA((8,)),
            pltpu.SemaphoreType.DMA((16,)),
        ],
        compiler_params=pltpu.CompilerParams(vmem_limit_bytes=60 << 20),
        cost_estimate=pl.CostEstimate(flops=1 << 20, bytes_accessed=1 << 16, transcendentals=0),
        name="up",
    )(place, *blocks, gain, *shards)


def down(hidden, shards):
    rows = jnp.concatenate(shards, axis=0)
    return lax.dot_general(hidden, rows, (((1,), (1,)), ((), ())), preferred_element_type=F32).astype(BF)


def tensor_sum(out):
    u = out.reshape(4, 128, out.shape[1])
    both = ring_sum([u[0], u[1], u[2], u[3]], ZP, ZM)
    other = go(both[64:].astype(BF), YHI)
    return both[:64] + other.astype(F32)


def ln_body(br0, br1, res, ls, gain, bias, out, held):
    total = jnp.zeros((64, 1), F32)
    for k in range(16):
        if k < FIRST:
            b = br0[:, k * 200 : k * 200 + 200]
        else:
            b = br1[:, (k - FIRST) * 200 : (k - FIRST) * 200 + 200]
        p = shard_place(k)
        v = (res[p].astype(F32) + ls[p] * b).astype(BF).astype(F32)
        held[p] = v
        total += jnp.sum(v, axis=1, keepdims=True)
    mean = (total[0:16] + total[16:32] + total[32:48] + total[48:64]) * (1.0 / 12800.0)
    mean = jnp.concatenate([mean] * 4, axis=0)
    total = jnp.zeros((64, 1), F32)
    for p in range(16):
        v = held[p] - mean
        total += jnp.sum(v * v, axis=1, keepdims=True)
    var = (total[0:16] + total[16:32] + total[32:48] + total[48:64]) * (1.0 / 12800.0)
    inv = jnp.concatenate([lax.rsqrt(var + 1e-05)] * 4, axis=0)
    for p in range(16):
        v = (held[p] - mean) * inv
        for q in range(4):
            piece = v[q * 16 : q * 16 + 16] * gain[q, p] + bias[q, p]
            out[q * 4 + p // 4, :, (p % 4) * 200 : (p % 4) * 200 + 200] = piece.astype(BF)


def layer_norm(parts, res, ls, gain, bias):
    return pl.pallas_call(
        ln_body,
        out_shape=jax.ShapeDtypeStruct((16, 16, 800), BF),
        in_specs=[VMEM] * 6,
        out_specs=VMEM,
        scratch_shapes=[pltpu.VMEM((16, 64, 200), F32)],
        compiler_params=pltpu.CompilerParams(vmem_limit_bytes=24 << 20),
        cost_estimate=pl.CostEstimate(flops=1 << 20, bytes_accessed=1 << 16, transcendentals=0),
        name="layer_norm",
    )(*parts, res, ls, gain, bias)


def proj_body(table, *refs):
    blocks, weight, out, held, lhs, sems = refs[:8], refs[8], refs[9], refs[10], refs[11], refs[12]
    copies = [pltpu.make_async_copy(blocks[i], held.at[pl.ds(i * 16, 16)], sems.at[i]) for i in range(8)]
    for cp in copies:
        cp.start()
    for cp in copies:
        cp.wait()

    def tile(m, _):
        for s in range(16):
            at = table[m * 16 + s]
            v = held[jnp.maximum(at, 0)]
            lhs[s * 16 : s * 16 + 16, :] = jnp.where(at >= 0, v, jnp.zeros_like(v))
        rows = pl.ds(pl.multiple_of(m * 256, 256), 256)
        out[rows, :] = jnp.dot(lhs[...], weight[...], preferred_element_type=F32).astype(BF)
        return 0

    lax.fori_loop(0, 8, tile, 0)


def proj(table, blocks, weight):
    return pl.pallas_call(
        proj_body,
        out_shape=jax.ShapeDtypeStruct((2048, 1024), BF),
        in_specs=[SMEM] + [ANY] * 8 + [VMEM],
        out_specs=VMEM,
        scratch_shapes=[pltpu.VMEM((128, 16, 800), BF), pltpu.VMEM((256, 800), BF), pltpu.SemaphoreType.DMA((8,))],
        compiler_params=pltpu.CompilerParams(vmem_limit_bytes=24 << 20),
        cost_estimate=pl.CostEstimate(flops=1 << 20, bytes_accessed=1 << 16, transcendentals=0),
        name="proj",
    )(table, *blocks, weight)


def shards(
    tokens,
    vit_gain,
    fc_up,
    fc_down,
    layer_scale,
    proj_gain,
    proj_bias,
    proj_in,
    proj_out,
    clip_frames,
    slot_perm,
):
    x, yl, c, z, yh = coords()

    frame_ids = jnp.arange(128, dtype=jnp.int32)
    inverse = jnp.sum(jnp.where(slot_perm[None, :] == frame_ids[:, None], frame_ids[None, :], 0), axis=1)
    place = frame_ids // 8
    owner = (flip(yl, (place // 4) % 2) * 4 + (x + place) % 4) * 2 + flip(c, place // 8)
    frame = inverse[owner * 8 + frame_ids % 8]
    te = frame % 8
    table = ((te // 2 - z + 4) % 4 * 2 + flip(te % 2, yh)) * 16 + frame // 8
    table = jnp.where(frame < clip_frames[0], table, -1).astype(jnp.int32)

    place = jnp.stack([shard_place(k) for k in range(16)]).astype(jnp.int32)

    t = tokens.reshape(8, 16, 4, 2, 200).transpose(3, 0, 2, 1, 4).reshape(2, 512, 200)
    uw, dw = fc_up, fc_down

    uo, do, uw, dw, t = phase(go(uw, CORE), go(dw, CORE), uw, dw, t)
    p, t_zm, t_zp, ua, uao, uw, dw, do, t = phase(
        go(t, YHI), go(t, ZP), go(t, ZM), go(uw, XBOTH), go(uo, XBOTH), uw, dw, do, t
    )
    uv, p_zm, p_zp, ue, da, t_zm, uao, ua, dw, do = phase(
        go(uw, YLO), go(p, ZP), go(p, ZM), go(ua, XBOTH), go(dw, XBOTH), t_zm, uao, ua, dw, do
    )
    ub, uf = go(uv, XBOTH), go(ue, YLO)
    uvo, t_zm, p_zp = phase(go(uv, CORE), t_zm, p_zp)
    ub, ubo, uf, t_z2, p_z2, uao, ua, ue, do, da, dw = phase(
        ub, go(uvo, XBOTH), uf, go(t_zm, ZP), go(p_zp, ZM), uao, ua, ue, do, da, dw
    )
    ua2, uao2, ue2 = go(ua, CORE), go(uao, CORE), go(ue, CORE)
    ub2, ubo2, uf2 = go(ub, CORE), go(ubo, CORE), go(uf, CORE)
    w_up = [uw, uo, uv, uvo, ua, ua2, uao, uao2, ue, ue2, ub, ub2, ubo, ubo2, uf, uf2]
    dao, de, dv, da, hidden, res = phase(
        go(do, XBOTH),
        go(da, XBOTH),
        go(dw, YLO),
        da,
        *up(place, [t, p, t_zp, p_zp, t_z2, p_z2, t_zm, p_zm], vit_gain.reshape(16, 1, 200), w_up),
    )
    db, df = go(dv, XBOTH), go(de, YLO)
    dvo, da, dao, de = phase(go(dv, CORE), da, dao, de)
    dbo = go(dvo, XBOTH)
    w_down = [dw, do, dv, dvo, da, go(da, CORE), dao, go(dao, CORE), de, go(de, CORE)]
    w_late = [db, go(db, CORE), dbo, go(dbo, CORE), df, go(df, CORE)]
    parts = [tensor_sum(down(hidden, w_down)), tensor_sum(down(hidden, w_late))]
    shuffled = layer_norm(
        parts,
        res,
        layer_scale.reshape(16, 1, 200),
        proj_gain.reshape(4, 16, 1, 200),
        proj_bias.reshape(4, 16, 1, 200),
    )
    spread = lax.all_to_all(shuffled, "dp", split_axis=0, concat_axis=0, tiled=True)
    partial = proj(table, gather_tensor(spread), proj_in).reshape(2, 8, 128, 1024)
    both = add(partial[0], go(partial[1], CORE)).astype(BF)
    part_a, part_b = both[:, :, :384], both[:, :, 384:]
    t = add(part_a[0:4], go(part_a[4:8], YLO)).astype(BF)
    pre_a = ring_sum([t[0], t[1], t[2], t[3]], XP, XM)
    u = [jnp.concatenate([part_b[d], part_b[4 + d]], axis=0) for d in range(4)]
    pair = ring_sum(u, XP, XM)
    pre_b = pair[:128] + go(pair[128:].astype(BF), YLO).astype(F32)

    pre = jnp.concatenate([pre_a, pre_b], axis=1)
    whole = jnp.dot(gelu(pre).astype(BF), proj_out, preferred_element_type=F32).astype(BF)
    terms = jnp.stack([lax.dynamic_slice_in_dim(whole, frame_of(r) * 1024, 1024, 1) for r in range(8)])
    terms = terms.reshape(4, 2, 128, 1024)
    part_a, part_b = terms[..., :384], terms[..., 384:]
    t = add(part_a[:, 0], go(part_a[:, 1], YHI)).astype(BF)
    out_a = ring_sum([t[0], t[1], t[2], t[3]], ZP, ZM)
    pair = ring_sum([part_b[d].reshape(256, 640) for d in range(4)], ZP, ZM)
    out_b = pair[:128] + go(pair[128:].astype(BF), YHI).astype(F32)
    return jnp.concatenate([out_a, out_b], axis=1).astype(BF)


def solution(mesh):
    return jax.shard_map(
        shards,
        mesh=mesh,
        in_specs=(
            P("dp", "tensor"),
            P(),
            P("dp", "tensor"),
            P("dp", "tensor"),
            P(),
            P(),
            P(),
            P("dp", "tensor"),
            P("tensor", None),
            P(),
            P(),
        ),
        out_specs=P("dp", "tensor"),
        check_vma=False,
    )
```

```python
import jax
import jax.numpy as jnp
from jax import lax
from jax.experimental import pallas as pl
from jax.experimental.pallas import tpu as pltpu
from jax.sharding import PartitionSpec as P

AXES = ("dp", "tensor")
BF = jnp.bfloat16
F32 = jnp.float32


def hop(move):
    pairs = []
    for yl in range(2):
        for x in range(4):
            for c in range(2):
                for z in range(4):
                    for yh in range(2):
                        x2, yl2, c2, z2, yh2 = move(x, yl, c, z, yh)
                        src = ((yl * 4 + x) * 2 + c) * 8 + z * 2 + yh
                        dst = ((yl2 * 4 + x2 % 4) * 2 + c2) * 8 + (z2 % 4) * 2 + yh2
                        pairs.append((src, dst))
    return pairs


CORE = hop(lambda x, yl, c, z, yh: (x, yl, 1 - c, z, yh))
YLO = hop(lambda x, yl, c, z, yh: (x, 1 - yl, c, z, yh))
YHI = hop(lambda x, yl, c, z, yh: (x, yl, c, z, 1 - yh))
XP = hop(lambda x, yl, c, z, yh: (x + 1, yl, c, z, yh))
XM = hop(lambda x, yl, c, z, yh: (x + 3, yl, c, z, yh))
ZP = hop(lambda x, yl, c, z, yh: (x, yl, c, z + 1, yh))
ZM = hop(lambda x, yl, c, z, yh: (x, yl, c, z + 3, yh))
XBOTH = hop(lambda x, yl, c, z, yh: (x + 1 + 2 * c, yl, c, z, yh))
ZBOTH = hop(lambda x, yl, c, z, yh: (x, yl, c, z + 1 + 2 * c, yh))


def go(a, pairs):
    return lax.ppermute(a, AXES, pairs)


def flip(a, d):
    return a + d - 2 * a * d


def coords():
    dp = lax.axis_index("dp")
    te = lax.axis_index("tensor")
    return (dp // 2) % 4, dp // 8, dp % 2, te // 2, te % 2


SHARDS = (
    (0, 0, 0),
    (0, 0, 1),
    (0, 1, 0),
    (0, 1, 1),
    (1, 0, 0),
    (-1, 0, 1),
    (1, 0, 1),
    (-1, 0, 0),
    (2, 0, 0),
    (2, 0, 1),
    (1, 1, 0),
    (-1, 1, 1),
    (1, 1, 1),
    (-1, 1, 0),
    (2, 1, 0),
    (2, 1, 1),
)
FIRST = 10


def shard_place(k):
    x, yl, c, _, _ = coords()
    step, dy, dc = SHARDS[k]
    if step == 2:
        dx = 2
    else:
        dx = step * (2 * c - 1) + 4
    return (flip(yl, dy) * 4 + (x + dx) % 4) * 2 + flip(c, dc)


def phase(*values):
    return lax.optimization_barrier(values)


def gather_tensor(a):
    zm_o, zp_o, p = phase(go(a, ZP), go(a, ZM), go(a, YHI))
    half = a.shape[0] // 2
    zm_p, zp_p = go(p, ZP), go(p, ZM)
    z2_o = jnp.concatenate([go(zm_o[:half], ZP), go(zp_o[half:], ZM)], axis=0)
    z2_p = go(z2_o, YHI)
    return [a, p, zp_o, zp_p, z2_o, z2_p, zm_o, zm_p]


def add(a, b):
    return a.astype(F32) + b.astype(F32)


def ring_first(u, plus, minus):
    half = u[2].shape[0] // 2
    return go(u[2][:half], plus), go(u[2][half:], minus)


def ring_second(u, up, down, plus, minus):
    half = u[2].shape[0] // 2
    first = jnp.concatenate([add(u[1][:half], up).astype(BF), u[1][half:]], axis=0)
    third = jnp.concatenate([u[3][:half], add(u[3][half:], down).astype(BF)], axis=0)
    first, third = phase(first, third)
    return go(first, plus), go(third, minus)


def ring_last(u, up, down):
    return u[0].astype(F32) + up.astype(F32) + down.astype(F32)


def ring_sum(u, plus, minus):
    up, down = phase(*ring_first(u, plus, minus))
    up, down = phase(*ring_second(u, up, down, plus, minus))
    return ring_last(u, up, down)


def gelu(v):
    return 0.5 * v * (1.0 + lax.erf(v * 0.7071067811865476))


ANY = pl.BlockSpec(memory_space=pl.ANY)
VMEM = pl.BlockSpec(memory_space=pltpu.VMEM)
SMEM = pl.BlockSpec(memory_space=pltpu.SMEM)


def frame_of(r):
    _, _, _, z, yh = coords()
    return ((z + r // 2) % 4) * 2 + flip(yh, r % 2)


def up_body(place, *refs):
    blocks, gain, shards = refs[:8], refs[8], refs[9:25]
    out, res, xs, scaled, held, squares, xsems, sems = refs[25:]
    xcopies = [
        pltpu.make_async_copy(blocks[i], xs.at[pl.ds(frame_of(i) * 2, 2)], xsems.at[i]) for i in range(8)
    ]
    copies = [pltpu.make_async_copy(shards[k], held.at[k], sems.at[k]) for k in range(16)]
    for cp in xcopies + copies:
        cp.start()
    squares[...] = jnp.zeros_like(squares)
    for cp in xcopies:
        cp.wait()

    def shard(k, _):
        p = place[k]
        for r in range(8):
            v = xs[p, pl.ds(pl.multiple_of(frame_of(r) * 64, 64), 64), :].astype(F32)
            squares[r * 64 : r * 64 + 64, :] += v * v
            scaled[k, r * 64 : r * 64 + 64, :] = (v * gain[p]).astype(BF)
        return 0

    lax.fori_loop(0, 16, shard, 0)
    scale = lax.rsqrt(jnp.sum(squares[...], axis=1, keepdims=True) * (1.0 / 3200.0) + 1e-06)
    own = pl.ds(pl.multiple_of(frame_of(0) * 64, 64), 64)
    for p in range(16):
        res[p] = xs[p, own, :]
    for cp in copies:
        cp.wait()
    for start in range(0, 1600, 256):
        end = min(start + 256, 1600)
        act = jnp.dot(scaled[0], held[0, :, start:end], preferred_element_type=F32)
        for k in range(1, 16):
            act += jnp.dot(scaled[k], held[k, :, start:end], preferred_element_type=F32)
        out[:, start:end] = gelu(act * scale).astype(BF)


def up(place, blocks, gain, shards):
    return pl.pallas_call(
        up_body,
        out_shape=(jax.ShapeDtypeStruct((512, 1600), BF), jax.ShapeDtypeStruct((16, 64, 200), BF)),
        in_specs=[SMEM] + [ANY] * 8 + [VMEM] + [ANY] * 16,
        out_specs=(VMEM, VMEM),
        scratch_shapes=[
            pltpu.VMEM((16, 512, 200), BF),
            pltpu.VMEM((16, 512, 200), BF),
            pltpu.VMEM((16, 200, 1600), BF),
            pltpu.VMEM((512, 200), F32),
            pltpu.SemaphoreType.DMA((8,)),
            pltpu.SemaphoreType.DMA((16,)),
        ],
        compiler_params=pltpu.CompilerParams(vmem_limit_bytes=60 << 20),
        cost_estimate=pl.CostEstimate(flops=1 << 20, bytes_accessed=1 << 16, transcendentals=0),
        name="up",
    )(place, *blocks, gain, *shards)


def down(hidden, shards):
    rows = jnp.concatenate(shards, axis=0)
    return lax.dot_general(hidden, rows, (((1,), (1,)), ((), ())), preferred_element_type=F32).astype(BF)


def ln_body(br0, br1, res, ls, gain, bias, out, held):
    total = jnp.zeros((64, 1), F32)
    for k in range(16):
        if k < FIRST:
            b = br0[:, k * 200 : k * 200 + 200]
        else:
            b = br1[:, (k - FIRST) * 200 : (k - FIRST) * 200 + 200]
        p = shard_place(k)
        v = (res[p].astype(F32) + ls[p] * b).astype(BF).astype(F32)
        held[p] = v
        total += jnp.sum(v, axis=1, keepdims=True)
    mean = (total[0:16] + total[16:32] + total[32:48] + total[48:64]) * (1.0 / 12800.0)
    mean = jnp.concatenate([mean] * 4, axis=0)
    total = jnp.zeros((64, 1), F32)
    for p in range(16):
        v = held[p] - mean
        total += jnp.sum(v * v, axis=1, keepdims=True)
    var = (total[0:16] + total[16:32] + total[32:48] + total[48:64]) * (1.0 / 12800.0)
    inv = jnp.concatenate([lax.rsqrt(var + 1e-05)] * 4, axis=0)
    for p in range(16):
        v = (held[p] - mean) * inv
        for q in range(4):
            piece = v[q * 16 : q * 16 + 16] * gain[q, p] + bias[q, p]
            out[q * 4 + p // 4, :, (p % 4) * 200 : (p % 4) * 200 + 200] = piece.astype(BF)


def layer_norm(parts, res, ls, gain, bias):
    return pl.pallas_call(
        ln_body,
        out_shape=jax.ShapeDtypeStruct((16, 16, 800), BF),
        in_specs=[VMEM] * 6,
        out_specs=VMEM,
        scratch_shapes=[pltpu.VMEM((16, 64, 200), F32)],
        compiler_params=pltpu.CompilerParams(vmem_limit_bytes=24 << 20),
        cost_estimate=pl.CostEstimate(flops=1 << 20, bytes_accessed=1 << 16, transcendentals=0),
        name="layer_norm",
    )(*parts, res, ls, gain, bias)


def arrange_body(table, *refs):
    blocks, out, held, sems = refs[:8], refs[8], refs[9], refs[10]
    copies = [pltpu.make_async_copy(blocks[i], held.at[pl.ds(i * 16, 16)], sems.at[i]) for i in range(8)]
    for cp in copies:
        cp.start()
    for cp in copies:
        cp.wait()

    def tile(m, _):
        for s in range(8):
            at = table[m * 8 + s]
            v = held[jnp.maximum(at, 0)]
            rows = pl.ds(pl.multiple_of(m * 128 + s * 16, 16), 16)
            out[rows, :] = jnp.where(at >= 0, v, jnp.zeros_like(v))
        return 0

    lax.fori_loop(0, 16, tile, 0)


def arrange(table, blocks):
    return pl.pallas_call(
        arrange_body,
        out_shape=jax.ShapeDtypeStruct((2048, 800), BF),
        in_specs=[SMEM] + [ANY] * 8,
        out_specs=VMEM,
        scratch_shapes=[pltpu.VMEM((128, 16, 800), BF), pltpu.SemaphoreType.DMA((8,))],
        compiler_params=pltpu.CompilerParams(vmem_limit_bytes=16 << 20),
        cost_estimate=pl.CostEstimate(flops=1 << 20, bytes_accessed=1 << 16, transcendentals=0),
        name="arrange",
    )(table, *blocks)


def shards(
    tokens,
    vit_gain,
    fc_up,
    fc_down,
    layer_scale,
    proj_gain,
    proj_bias,
    proj_in,
    proj_out,
    clip_frames,
    slot_perm,
):
    x, yl, c, z, yh = coords()

    frame_ids = jnp.arange(128, dtype=jnp.int32)
    inverse = jnp.sum(jnp.where(slot_perm[None, :] == frame_ids[:, None], frame_ids[None, :], 0), axis=1)
    place = frame_ids // 8
    owner = (flip(yl, place % 2) * 4 + (x + place // 2) % 4) * 2 + flip(c, place // 8)
    frame = inverse[owner * 8 + frame_ids % 8]
    te = frame % 8
    table = ((te // 2 - z + 4) % 4 * 2 + flip(te % 2, yh)) * 16 + frame // 8
    table = jnp.where(frame < clip_frames[0], table, -1).astype(jnp.int32)

    place = jnp.stack([shard_place(k) for k in range(16)]).astype(jnp.int32)

    t = tokens.reshape(8, 16, 4, 2, 200).transpose(3, 0, 2, 1, 4).reshape(2, 512, 200)
    uw, dw = fc_up, fc_down

    ua = go(uw, XBOTH)
    uo, do, uw, dw, t = phase(go(uw, CORE), go(dw, CORE), uw, dw, t)
    p, t_zm, t_zp, ua, uao, uw, dw, do, t = phase(
        go(t, YHI), go(t, ZP), go(t, ZM), ua, go(uo, XBOTH), uw, dw, do, t
    )
    uv, p_zm, p_zp, ue, da, t_zm, uao, ua, dw, do = phase(
        go(uw, YLO), go(p, ZP), go(p, ZM), go(ua, XBOTH), go(dw, XBOTH), t_zm, uao, ua, dw, do
    )
    ub, uf = go(uv, XBOTH), go(ue, YLO)
    uvo, ua2, uao2, ue2, ua, uao, ue, t_zm, p_zp = phase(
        go(uv, CORE), go(ua, CORE), go(uao, CORE), go(ue, CORE), ua, uao, ue, t_zm, p_zp
    )
    ub, ubo, uf, t_z2, p_z2, uao, ua, ue, do, da, dw = phase(
        ub, go(uvo, XBOTH), uf, go(t_zm, ZP), go(p_zp, ZM), uao, ua, ue, do, da, dw
    )
    ub2, ubo2, uf2 = go(ub, CORE), go(ubo, CORE), go(uf, CORE)
    w_up = [uw, uo, uv, uvo, ua, ua2, uao, uao2, ue, ue2, ub, ub2, ubo, ubo2, uf, uf2]
    dao, de, dv, da, hidden, res = phase(
        go(do, XBOTH),
        go(da, XBOTH),
        go(dw, YLO),
        da,
        *up(place, [t, p, t_zp, p_zp, t_z2, p_z2, t_zm, p_zm], vit_gain.reshape(16, 1, 200), w_up),
    )
    db, df = go(dv, XBOTH), go(de, YLO)
    dvo, da2, dao2, de2, da, dao, de, hidden = phase(
        go(dv, CORE), go(da, CORE), go(dao, CORE), go(de, CORE), da, dao, de, hidden
    )
    early = down(hidden, [dw, do, dv, dvo, da, da2, dao, dao2, de, de2]).reshape(4, 128, 2000)
    db, dbo, df, up_e, down_e, hidden = phase(db, go(dvo, XBOTH), df, *ring_first(early, ZP, ZM), hidden)
    db2, dbo2, df2 = go(db, CORE), go(dbo, CORE), go(df, CORE)
    up_e, down_e = ring_second(early, up_e, down_e, ZP, ZM)
    late = down(hidden, [db, db2, dbo, dbo2, df, df2]).reshape(4, 128, 1200)
    up_e, down_e = phase(up_e, down_e)
    both_e = ring_last(early, up_e, down_e)
    other_e = go(both_e[64:].astype(BF), YHI)
    both_l = ring_sum(late, ZP, ZM)
    other_l = go(both_l[64:].astype(BF), YHI)
    parts = [both_e[:64] + other_e.astype(F32), both_l[:64] + other_l.astype(F32)]
    shuffled = layer_norm(
        parts,
        res,
        layer_scale.reshape(16, 1, 200),
        proj_gain.reshape(4, 16, 1, 200),
        proj_bias.reshape(4, 16, 1, 200),
    )
    spread = lax.all_to_all(shuffled, "dp", split_axis=0, concat_axis=0, tiled=True)
    rows = arrange(table, gather_tensor(spread))
    theirs = jnp.dot(rows[1024:], proj_in, preferred_element_type=F32).astype(BF)
    ours, theirs = phase(jnp.dot(rows[:1024], proj_in, preferred_element_type=F32).astype(BF), go(theirs, CORE))
    both = add(ours, theirs).astype(BF)
    pair = ring_sum(both.reshape(4, 256, 1024), XP, XM)
    pre = pair[:128] + go(pair[128:].astype(BF), YLO).astype(F32)

    (act,) = phase(gelu(pre).astype(BF))
    terms = [None] * 4
    for dz in (2, 1, 3, 0):
        weight = lax.dynamic_slice_in_dim(proj_out, (z + dz) % 4 * 2048, 2048, 1)
        term = jnp.dot(act, weight, preferred_element_type=F32).astype(BF)
        halves = [lax.dynamic_slice_in_dim(term, flip(yh, d) * 1024, 1024, 1) for d in range(2)]
        terms[dz] = jnp.concatenate(halves, axis=0)
    pair = ring_sum(terms, ZP, ZM)
    return (pair[:128] + go(pair[128:].astype(BF), YHI).astype(F32)).astype(BF)


def solution(mesh):
    return jax.shard_map(
        shards,
        mesh=mesh,
        in_specs=(
            P("dp", "tensor"),
            P(),
            P("dp", "tensor"),
            P("dp", "tensor"),
            P(),
            P(),
            P(),
            P("dp", "tensor"),
            P("tensor", None),
            P(),
            P(),
        ),
        out_specs=P("dp", "tensor"),
        check_vma=False,
    )
```

```python
import jax
import jax.numpy as jnp
from jax import lax
from jax.experimental import pallas as pl
from jax.experimental.pallas import tpu as pltpu
from jax.sharding import PartitionSpec as P

AXES = ("dp", "tensor")
BF = jnp.bfloat16
F32 = jnp.float32


def hop(move):
    pairs = []
    for yl in range(2):
        for x in range(4):
            for c in range(2):
                for z in range(4):
                    for yh in range(2):
                        x2, yl2, c2, z2, yh2 = move(x, yl, c, z, yh)
                        src = ((yl * 4 + x) * 2 + c) * 8 + z * 2 + yh
                        dst = ((yl2 * 4 + x2 % 4) * 2 + c2) * 8 + (z2 % 4) * 2 + yh2
                        pairs.append((src, dst))
    return pairs


CORE = hop(lambda x, yl, c, z, yh: (x, yl, 1 - c, z, yh))
YLO = hop(lambda x, yl, c, z, yh: (x, 1 - yl, c, z, yh))
YHI = hop(lambda x, yl, c, z, yh: (x, yl, c, z, 1 - yh))
XP = hop(lambda x, yl, c, z, yh: (x + 1, yl, c, z, yh))
XM = hop(lambda x, yl, c, z, yh: (x + 3, yl, c, z, yh))
ZP = hop(lambda x, yl, c, z, yh: (x, yl, c, z + 1, yh))
ZM = hop(lambda x, yl, c, z, yh: (x, yl, c, z + 3, yh))
XBOTH = hop(lambda x, yl, c, z, yh: (x + 1 + 2 * c, yl, c, z, yh))
ZBOTH = hop(lambda x, yl, c, z, yh: (x, yl, c, z + 1 + 2 * c, yh))


def go(a, pairs):
    return lax.ppermute(a, AXES, pairs)


def flip(a, d):
    return a + d - 2 * a * d


def coords():
    dp = lax.axis_index("dp")
    te = lax.axis_index("tensor")
    return (dp // 2) % 4, dp // 8, dp % 2, te // 2, te % 2


SHARDS = (
    (0, 0, 0),
    (0, 0, 1),
    (0, 1, 0),
    (0, 1, 1),
    (1, 0, 0),
    (-1, 0, 1),
    (1, 0, 1),
    (-1, 0, 0),
    (2, 0, 0),
    (2, 0, 1),
    (1, 1, 0),
    (-1, 1, 1),
    (1, 1, 1),
    (-1, 1, 0),
    (2, 1, 0),
    (2, 1, 1),
)
FIRST = 10


def shard_place(k):
    x, yl, c, _, _ = coords()
    step, dy, dc = SHARDS[k]
    if step == 2:
        dx = 2
    else:
        dx = step * (2 * c - 1) + 4
    return (flip(yl, dy) * 4 + (x + dx) % 4) * 2 + flip(c, dc)


def phase(*values):
    return lax.optimization_barrier(values)


def gather_tensor(a):
    half = a.shape[0] // 2
    zm_o, zp_o = go(a, ZP), go(a, ZM)
    z2_o = jnp.concatenate([go(zm_o[:half], ZP), go(zp_o[half:], ZM)], axis=0)
    _, _, p = phase(zm_o, zp_o, go(a, YHI))
    zm_p, zp_p = go(p, ZP), go(p, ZM)
    z2_p = go(z2_o, YHI)
    return [a, p, zp_o, zp_p, z2_o, z2_p, zm_o, zm_p]


def add(a, b):
    return a.astype(F32) + b.astype(F32)


def ring_first(u, plus, minus):
    half = u[2].shape[0] // 2
    return go(u[2][:half], plus), go(u[2][half:], minus)


def ring_second(u, up, down, plus, minus):
    half = u[2].shape[0] // 2
    first = jnp.concatenate([add(u[1][:half], up).astype(BF), u[1][half:]], axis=0)
    third = jnp.concatenate([u[3][:half], add(u[3][half:], down).astype(BF)], axis=0)
    first, third = phase(first, third)
    return go(first, plus), go(third, minus)


def ring_last(u, up, down):
    return u[0].astype(F32) + up.astype(F32) + down.astype(F32)


def ring_sum(u, plus, minus):
    up, down = phase(*ring_first(u, plus, minus))
    up, down = phase(*ring_second(u, up, down, plus, minus))
    return ring_last(u, up, down)


def gelu(v):
    return 0.5 * v * (1.0 + lax.erf(v * 0.7071067811865476))


ANY = pl.BlockSpec(memory_space=pl.ANY)
VMEM = pl.BlockSpec(memory_space=pltpu.VMEM)
SMEM = pl.BlockSpec(memory_space=pltpu.SMEM)


def frame_of(r):
    _, _, _, z, yh = coords()
    return ((z + r // 2) % 4) * 2 + flip(yh, r % 2)


def up_body(place, *refs):
    blocks, gain, shards = refs[:8], refs[8], refs[9:25]
    out, res, xs, scaled, held, squares, xsems, sems = refs[25:]
    xcopies = [
        pltpu.make_async_copy(blocks[i], xs.at[pl.ds(frame_of(i) * 2, 2)], xsems.at[i]) for i in range(8)
    ]
    copies = [pltpu.make_async_copy(shards[k], held.at[k], sems.at[k]) for k in range(16)]
    for cp in xcopies + copies:
        cp.start()
    squares[...] = jnp.zeros_like(squares)
    for cp in xcopies:
        cp.wait()

    def shard(k, _):
        p = place[k]
        for r in range(8):
            v = xs[p, pl.ds(pl.multiple_of(frame_of(r) * 64, 64), 64), :].astype(F32)
            squares[r * 64 : r * 64 + 64, :] += v * v
            scaled[k, r * 64 : r * 64 + 64, :] = (v * gain[p]).astype(BF)
        return 0

    lax.fori_loop(0, 16, shard, 0)
    scale = lax.rsqrt(jnp.sum(squares[...], axis=1, keepdims=True) * (1.0 / 3200.0) + 1e-06)
    own = pl.ds(pl.multiple_of(frame_of(0) * 64, 64), 64)
    for p in range(16):
        res[p] = xs[p, own, :]
    for cp in copies:
        cp.wait()
    for start in range(0, 1600, 256):
        end = min(start + 256, 1600)
        act = jnp.dot(scaled[0], held[0, :, start:end], preferred_element_type=F32)
        for k in range(1, 16):
            act += jnp.dot(scaled[k], held[k, :, start:end], preferred_element_type=F32)
        out[:, start:end] = gelu(act * scale).astype(BF)


def up(place, blocks, gain, shards):
    return pl.pallas_call(
        up_body,
        out_shape=(jax.ShapeDtypeStruct((512, 1600), BF), jax.ShapeDtypeStruct((16, 64, 200), BF)),
        in_specs=[SMEM] + [ANY] * 8 + [VMEM] + [ANY] * 16,
        out_specs=(VMEM, VMEM),
        scratch_shapes=[
            pltpu.VMEM((16, 512, 200), BF),
            pltpu.VMEM((16, 512, 200), BF),
            pltpu.VMEM((16, 200, 1600), BF),
            pltpu.VMEM((512, 200), F32),
            pltpu.SemaphoreType.DMA((8,)),
            pltpu.SemaphoreType.DMA((16,)),
        ],
        compiler_params=pltpu.CompilerParams(vmem_limit_bytes=28 << 20),
        cost_estimate=pl.CostEstimate(flops=1 << 20, bytes_accessed=1 << 16, transcendentals=0),
        name="up",
    )(place, *blocks, gain, *shards)


def down(hidden, shards):
    rows = jnp.concatenate(shards, axis=0)
    return lax.dot_general(hidden, rows, (((1,), (1,)), ((), ())), preferred_element_type=F32).astype(BF)


def ln_body(br0, br1, res, ls, gain, bias, out, held):
    total = jnp.zeros((64, 1), F32)
    for k in range(16):
        if k < FIRST:
            b = br0[:, k * 200 : k * 200 + 200]
        else:
            b = br1[:, (k - FIRST) * 200 : (k - FIRST) * 200 + 200]
        p = shard_place(k)
        v = (res[p].astype(F32) + ls[p] * b).astype(BF).astype(F32)
        held[p] = v
        total += jnp.sum(v, axis=1, keepdims=True)
    mean = (total[0:16] + total[16:32] + total[32:48] + total[48:64]) * (1.0 / 12800.0)
    mean = jnp.concatenate([mean] * 4, axis=0)
    total = jnp.zeros((64, 1), F32)
    for p in range(16):
        v = held[p] - mean
        total += jnp.sum(v * v, axis=1, keepdims=True)
    var = (total[0:16] + total[16:32] + total[32:48] + total[48:64]) * (1.0 / 12800.0)
    inv = jnp.concatenate([lax.rsqrt(var + 1e-05)] * 4, axis=0)
    for p in range(16):
        v = (held[p] - mean) * inv
        for q in range(4):
            piece = v[q * 16 : q * 16 + 16] * gain[q, p] + bias[q, p]
            out[q * 4 + p // 4, :, (p % 4) * 200 : (p % 4) * 200 + 200] = piece.astype(BF)


def layer_norm(parts, res, ls, gain, bias):
    return pl.pallas_call(
        ln_body,
        out_shape=jax.ShapeDtypeStruct((16, 16, 800), BF),
        in_specs=[VMEM] * 6,
        out_specs=VMEM,
        scratch_shapes=[pltpu.VMEM((16, 64, 200), F32)],
        compiler_params=pltpu.CompilerParams(vmem_limit_bytes=8 << 20),
        cost_estimate=pl.CostEstimate(flops=1 << 20, bytes_accessed=1 << 16, transcendentals=0),
        name="layer_norm",
    )(*parts, res, ls, gain, bias)


def arrange_body(table, *refs):
    blocks, out, held, sems = refs[:8], refs[8], refs[9], refs[10]
    copies = [pltpu.make_async_copy(blocks[i], held.at[pl.ds(i * 16, 16)], sems.at[i]) for i in range(8)]
    for cp in copies:
        cp.start()
    for cp in copies:
        cp.wait()

    def tile(m, _):
        for s in range(8):
            at = table[m * 8 + s]
            v = held[jnp.maximum(at, 0)]
            rows = pl.ds(pl.multiple_of(m * 128 + s * 16, 16), 16)
            out[rows, :] = jnp.where(at >= 0, v, jnp.zeros_like(v))
        return 0

    lax.fori_loop(0, 16, tile, 0)


def arrange(table, blocks):
    return pl.pallas_call(
        arrange_body,
        out_shape=jax.ShapeDtypeStruct((2048, 800), BF),
        in_specs=[SMEM] + [ANY] * 8,
        out_specs=VMEM,
        scratch_shapes=[pltpu.VMEM((128, 16, 800), BF), pltpu.SemaphoreType.DMA((8,))],
        compiler_params=pltpu.CompilerParams(vmem_limit_bytes=10 << 20),
        cost_estimate=pl.CostEstimate(flops=1 << 20, bytes_accessed=1 << 16, transcendentals=0),
        name="arrange",
    )(table, *blocks)


def shards(
    tokens,
    vit_gain,
    fc_up,
    fc_down,
    layer_scale,
    proj_gain,
    proj_bias,
    proj_in,
    proj_out,
    clip_frames,
    slot_perm,
):
    x, yl, c, z, yh = coords()

    frame_ids = jnp.arange(128, dtype=jnp.int32)
    inverse = jnp.sum(jnp.where(slot_perm[None, :] == frame_ids[:, None], frame_ids[None, :], 0), axis=1)
    place = frame_ids // 8
    owner = (flip(yl, place % 2) * 4 + (x + place // 2) % 4) * 2 + flip(c, place // 8)
    frame = inverse[owner * 8 + frame_ids % 8]
    te = frame % 8
    table = ((te // 2 - z + 4) % 4 * 2 + flip(te % 2, yh)) * 16 + frame // 8
    table = jnp.where(frame < clip_frames[0], table, -1).astype(jnp.int32)

    place = jnp.stack([shard_place(k) for k in range(16)]).astype(jnp.int32)

    t = tokens.reshape(8, 16, 4, 2, 200).transpose(3, 0, 2, 1, 4).reshape(2, 512, 200)
    uw, dw = fc_up, fc_down

    ua = go(uw, XBOTH)
    uo, do, uw, dw, t, place, norm_gain = phase(
        go(uw, CORE), go(dw, CORE), uw, dw, t, place, vit_gain.reshape(16, 1, 200)
    )
    p, t_zm, t_zp, ua, uao, uw, dw, do, t = phase(
        go(t, YHI), go(t, ZP), go(t, ZM), ua, go(uo, XBOTH), uw, dw, do, t
    )
    uv, p_zm, p_zp, ue, da, t_zm, uao, ua, dw, do = phase(
        go(uw, YLO), go(p, ZP), go(p, ZM), go(ua, XBOTH), go(dw, XBOTH), t_zm, uao, ua, dw, do
    )
    ub, uf = go(uv, XBOTH), go(ue, YLO)
    uvo, ua2, uao2, ue2, ua, uao, ue, t_zm, p_zp = phase(
        go(uv, CORE), go(ua, CORE), go(uao, CORE), go(ue, CORE), ua, uao, ue, t_zm, p_zp
    )
    ub, ubo, uf, t_z2, p_z2, uao, ua, ue, do, da, dw = phase(
        ub, go(uvo, XBOTH), uf, go(t_zm, ZP), go(p_zp, ZM), uao, ua, ue, do, da, dw
    )
    ub2, ubo2, uf2 = go(ub, CORE), go(ubo, CORE), go(uf, CORE)
    w_up = [uw, uo, uv, uvo, ua, ua2, uao, uao2, ue, ue2, ub, ub2, ubo, ubo2, uf, uf2]
    dao, de, dv, da, hidden, res = phase(
        go(do, XBOTH),
        go(da, XBOTH),
        go(dw, YLO),
        da,
        *up(place, [t, p, t_zp, p_zp, t_z2, p_z2, t_zm, p_zm], norm_gain, w_up),
    )
    db, df = go(dv, XBOTH), go(de, YLO)
    dvo, da2, dao2, de2, da, dao, de, hidden = phase(
        go(dv, CORE), go(da, CORE), go(dao, CORE), go(de, CORE), da, dao, de, hidden
    )
    early = down(hidden, [dw, do, dv, dvo, da, da2, dao, dao2, de, de2]).reshape(4, 128, 2000)
    db, dbo, df, up_e, down_e, hidden = phase(db, go(dvo, XBOTH), df, *ring_first(early, ZP, ZM), hidden)
    db2, dbo2, df2 = go(db, CORE), go(dbo, CORE), go(df, CORE)
    up_e, down_e = ring_second(early, up_e, down_e, ZP, ZM)
    late = down(hidden, [db, db2, dbo, dbo2, df, df2]).reshape(4, 128, 1200)
    up_e, down_e = phase(up_e, down_e)
    both_e = ring_last(early, up_e, down_e)
    other_e = go(both_e[64:].astype(BF), YHI)
    both_l = ring_sum(late, ZP, ZM)
    other_l = go(both_l[64:].astype(BF), YHI)
    parts = [both_e[:64] + other_e.astype(F32), both_l[:64] + other_l.astype(F32)]
    shuffled = layer_norm(
        parts,
        res,
        layer_scale.reshape(16, 1, 200),
        proj_gain.reshape(4, 16, 1, 200),
        proj_bias.reshape(4, 16, 1, 200),
    )
    spread = lax.all_to_all(shuffled, "dp", split_axis=0, concat_axis=0, tiled=True)
    rows = arrange(table, gather_tensor(spread))
    theirs = jnp.dot(rows[1024:], proj_in, preferred_element_type=F32).astype(BF)
    ours, theirs = phase(jnp.dot(rows[:1024], proj_in, preferred_element_type=F32).astype(BF), go(theirs, CORE))
    both = add(ours, theirs).astype(BF)
    pair = ring_sum(both.reshape(4, 256, 1024), XP, XM)
    pre = pair[:128] + go(pair[128:].astype(BF), YLO).astype(F32)

    (act,) = phase(gelu(pre).astype(BF))
    terms = [None] * 4
    for dz in (2, 1, 3, 0):
        if dz == 1:
            terms[2], act = phase(terms[2], act)
        weight = lax.dynamic_slice_in_dim(proj_out, (z + dz) % 4 * 2048, 2048, 1)
        term = jnp.dot(act, weight, preferred_element_type=F32).astype(BF)
        halves = [lax.dynamic_slice_in_dim(term, flip(yh, d) * 1024, 1024, 1) for d in range(2)]
        terms[dz] = jnp.concatenate(halves, axis=0)
    pair = ring_sum(terms, ZP, ZM)
    return (pair[:128] + go(pair[128:].astype(BF), YHI).astype(F32)).astype(BF)


def solution(mesh):
    return jax.shard_map(
        shards,
        mesh=mesh,
        in_specs=(
            P("dp", "tensor"),
            P(),
            P("dp", "tensor"),
            P("dp", "tensor"),
            P(),
            P(),
            P(),
            P("dp", "tensor"),
            P("tensor", None),
            P(),
            P(),
        ),
        out_specs=P("dp", "tensor"),
        check_vma=False,
    )
```

```python
import jax
import jax.numpy as jnp
from jax import lax
from jax.experimental import pallas as pl
from jax.experimental.pallas import tpu as pltpu
from jax.sharding import PartitionSpec as P

AXES = ("dp", "tensor")
BF = jnp.bfloat16
F32 = jnp.float32


def hop(move):
    pairs = []
    for yl in range(2):
        for x in range(4):
            for c in range(2):
                for z in range(4):
                    for yh in range(2):
                        x2, yl2, c2, z2, yh2 = move(x, yl, c, z, yh)
                        src = ((yl * 4 + x) * 2 + c) * 8 + z * 2 + yh
                        dst = ((yl2 * 4 + x2 % 4) * 2 + c2) * 8 + (z2 % 4) * 2 + yh2
                        pairs.append((src, dst))
    return pairs


CORE = hop(lambda x, yl, c, z, yh: (x, yl, 1 - c, z, yh))
YLO = hop(lambda x, yl, c, z, yh: (x, 1 - yl, c, z, yh))
YHI = hop(lambda x, yl, c, z, yh: (x, yl, c, z, 1 - yh))
XP = hop(lambda x, yl, c, z, yh: (x + 1, yl, c, z, yh))
XM = hop(lambda x, yl, c, z, yh: (x + 3, yl, c, z, yh))
ZP = hop(lambda x, yl, c, z, yh: (x, yl, c, z + 1, yh))
ZM = hop(lambda x, yl, c, z, yh: (x, yl, c, z + 3, yh))
XBOTH = hop(lambda x, yl, c, z, yh: (x + 1 + 2 * c, yl, c, z, yh))
ZBOTH = hop(lambda x, yl, c, z, yh: (x, yl, c, z + 1 + 2 * c, yh))


def go(a, pairs):
    return lax.ppermute(a, AXES, pairs)


def flip(a, d):
    return a + d - 2 * a * d


def coords():
    dp = lax.axis_index("dp")
    te = lax.axis_index("tensor")
    return (dp // 2) % 4, dp // 8, dp % 2, te // 2, te % 2


SHARDS = (
    (0, 0, 0),
    (0, 0, 1),
    (0, 1, 0),
    (0, 1, 1),
    (1, 0, 0),
    (-1, 0, 1),
    (1, 0, 1),
    (-1, 0, 0),
    (2, 0, 0),
    (2, 0, 1),
    (1, 1, 0),
    (-1, 1, 1),
    (1, 1, 1),
    (-1, 1, 0),
    (2, 1, 0),
    (2, 1, 1),
)
FIRST = 10


def shard_place(k):
    x, yl, c, _, _ = coords()
    step, dy, dc = SHARDS[k]
    if step == 2:
        dx = 2
    else:
        dx = step * (2 * c - 1) + 4
    return (flip(yl, dy) * 4 + (x + dx) % 4) * 2 + flip(c, dc)


def phase(*values):
    return lax.optimization_barrier(values)


def gather_tensor(a):
    half = a.shape[0] // 2
    p, zm_o, zp_o = go(a, YHI), go(a, ZP), go(a, ZM)
    upper, lower, p = phase(go(zm_o[:half], ZP), go(zp_o[half:], ZM), p)
    z2_o, p = phase(jnp.concatenate([upper, lower], axis=0), p)
    z2_p, zm_p, zp_p = phase(go(z2_o, YHI), go(p, ZP), go(p, ZM))
    return [a, p, zp_o, zp_p, z2_o, z2_p, zm_o, zm_p]


def add(a, b):
    return a.astype(F32) + b.astype(F32)


def ring_first(u, plus, minus):
    half = u[2].shape[0] // 2
    return go(u[2][:half], plus), go(u[2][half:], minus)


def ring_second(u, up, down, plus, minus):
    half = u[2].shape[0] // 2
    first = jnp.concatenate([add(u[1][:half], up).astype(BF), u[1][half:]], axis=0)
    third = jnp.concatenate([u[3][:half], add(u[3][half:], down).astype(BF)], axis=0)
    first, third = phase(first, third)
    return go(first, plus), go(third, minus)


def ring_last(u, up, down):
    return u[0].astype(F32) + up.astype(F32) + down.astype(F32)


def ring_sum(u, plus, minus):
    up, down = phase(*ring_first(u, plus, minus))
    up, down = phase(*ring_second(u, up, down, plus, minus))
    return ring_last(u, up, down)


def gelu(v):
    return 0.5 * v * (1.0 + lax.erf(v * 0.7071067811865476))


ANY = pl.BlockSpec(memory_space=pl.ANY)
VMEM = pl.BlockSpec(memory_space=pltpu.VMEM)
SMEM = pl.BlockSpec(memory_space=pltpu.SMEM)


def frame_of(r):
    _, _, _, z, yh = coords()
    return ((z + r // 2) % 4) * 2 + flip(yh, r % 2)


def up_body(place, *refs):
    blocks, gain, shards = refs[:8], refs[8], refs[9:25]
    out, res, xs, scaled, held, squares, xsems, sems = refs[25:]
    xcopies = [
        pltpu.make_async_copy(blocks[i], xs.at[pl.ds(frame_of(i) * 2, 2)], xsems.at[i]) for i in range(8)
    ]
    copies = [pltpu.make_async_copy(shards[k], held.at[k], sems.at[k]) for k in range(16)]
    for cp in xcopies + copies:
        cp.start()
    squares[...] = jnp.zeros_like(squares)
    for cp in xcopies:
        cp.wait()

    def shard(k, _):
        p = place[k]
        for r in range(8):
            v = xs[p, pl.ds(pl.multiple_of(frame_of(r) * 64, 64), 64), :].astype(F32)
            squares[r * 64 : r * 64 + 64, :] += v * v
            scaled[k, r * 64 : r * 64 + 64, :] = (v * gain[p]).astype(BF)
        return 0

    lax.fori_loop(0, 16, shard, 0)
    scale = lax.rsqrt(jnp.sum(squares[...], axis=1, keepdims=True) * (1.0 / 3200.0) + 1e-06)
    own = pl.ds(pl.multiple_of(frame_of(0) * 64, 64), 64)
    for p in range(16):
        res[p] = xs[p, own, :]
    for cp in copies:
        cp.wait()
    for start in range(0, 1600, 256):
        end = min(start + 256, 1600)
        act = jnp.dot(scaled[0], held[0, :, start:end], preferred_element_type=F32)
        for k in range(1, 16):
            act += jnp.dot(scaled[k], held[k, :, start:end], preferred_element_type=F32)
        out[:, start:end] = gelu(act * scale).astype(BF)


def up(place, blocks, gain, shards):
    return pl.pallas_call(
        up_body,
        out_shape=(jax.ShapeDtypeStruct((512, 1600), BF), jax.ShapeDtypeStruct((16, 64, 200), BF)),
        in_specs=[SMEM] + [ANY] * 8 + [VMEM] + [ANY] * 16,
        out_specs=(VMEM, VMEM),
        scratch_shapes=[
            pltpu.VMEM((16, 512, 200), BF),
            pltpu.VMEM((16, 512, 200), BF),
            pltpu.VMEM((16, 200, 1600), BF),
            pltpu.VMEM((512, 200), F32),
            pltpu.SemaphoreType.DMA((8,)),
            pltpu.SemaphoreType.DMA((16,)),
        ],
        compiler_params=pltpu.CompilerParams(vmem_limit_bytes=28 << 20),
        cost_estimate=pl.CostEstimate(flops=1 << 20, bytes_accessed=1 << 16, transcendentals=0),
        name="up",
    )(place, *blocks, gain, *shards)


def down(hidden, shards):
    rows = jnp.concatenate(shards, axis=0)
    return lax.dot_general(hidden, rows, (((1,), (1,)), ((), ())), preferred_element_type=F32).astype(BF)


def ln_body(br0, br1, res, ls, gain, bias, out, held):
    total = jnp.zeros((64, 1), F32)
    for k in range(16):
        if k < FIRST:
            b = br0[:, k * 200 : k * 200 + 200]
        else:
            b = br1[:, (k - FIRST) * 200 : (k - FIRST) * 200 + 200]
        p = shard_place(k)
        v = (res[p].astype(F32) + ls[p] * b).astype(BF).astype(F32)
        held[p] = v
        total += jnp.sum(v, axis=1, keepdims=True)
    mean = (total[0:16] + total[16:32] + total[32:48] + total[48:64]) * (1.0 / 12800.0)
    mean = jnp.concatenate([mean] * 4, axis=0)
    total = jnp.zeros((64, 1), F32)
    for p in range(16):
        v = held[p] - mean
        total += jnp.sum(v * v, axis=1, keepdims=True)
    var = (total[0:16] + total[16:32] + total[32:48] + total[48:64]) * (1.0 / 12800.0)
    inv = jnp.concatenate([lax.rsqrt(var + 1e-05)] * 4, axis=0)
    for p in range(16):
        v = (held[p] - mean) * inv
        for q in range(4):
            piece = v[q * 16 : q * 16 + 16] * gain[q, p] + bias[q, p]
            out[q * 4 + p // 4, :, (p % 4) * 200 : (p % 4) * 200 + 200] = piece.astype(BF)


def layer_norm(parts, res, ls, gain, bias):
    return pl.pallas_call(
        ln_body,
        out_shape=jax.ShapeDtypeStruct((16, 16, 800), BF),
        in_specs=[VMEM] * 6,
        out_specs=VMEM,
        scratch_shapes=[pltpu.VMEM((16, 64, 200), F32)],
        compiler_params=pltpu.CompilerParams(vmem_limit_bytes=8 << 20),
        cost_estimate=pl.CostEstimate(flops=1 << 20, bytes_accessed=1 << 16, transcendentals=0),
        name="layer_norm",
    )(*parts, res, ls, gain, bias)


def arrange_body(table, *refs):
    n = len(refs) - 3
    blocks, out, held, sems = refs[:n], refs[n], refs[n + 1], refs[n + 2]
    copies, at = [], 0
    for i in range(n):
        size = blocks[i].shape[0]
        copies.append(pltpu.make_async_copy(blocks[i], held.at[pl.ds(at, size)], sems.at[i]))
        at += size
    for cp in copies:
        cp.start()
    for cp in copies:
        cp.wait()

    def tile(m, _):
        for s in range(8):
            at = table[m * 8 + s]
            v = held[jnp.maximum(at, 0)]
            rows = pl.ds(pl.multiple_of(m * 128 + s * 16, 16), 16)
            out[rows, :] = jnp.where(at >= 0, v, jnp.zeros_like(v))
        return 0

    lax.fori_loop(0, table.shape[0] // 8, tile, 0)


def arrange(table, blocks):
    frames, rows, width = sum(b.shape[0] for b in blocks), blocks[0].shape[1], blocks[0].shape[2]
    return pl.pallas_call(
        arrange_body,
        out_shape=jax.ShapeDtypeStruct((table.shape[0] * rows, width), BF),
        in_specs=[SMEM] + [ANY] * len(blocks),
        out_specs=VMEM,
        scratch_shapes=[pltpu.VMEM((frames, rows, width), BF), pltpu.SemaphoreType.DMA((len(blocks),))],
        compiler_params=pltpu.CompilerParams(vmem_limit_bytes=10 << 20),
        cost_estimate=pl.CostEstimate(flops=1 << 20, bytes_accessed=1 << 16, transcendentals=0),
        name="arrange",
    )(table, *blocks)


def shards(
    tokens,
    vit_gain,
    fc_up,
    fc_down,
    layer_scale,
    proj_gain,
    proj_bias,
    proj_in,
    proj_out,
    clip_frames,
    slot_perm,
):
    x, yl, c, z, yh = coords()

    frame_ids = jnp.arange(128, dtype=jnp.int32)
    inverse = jnp.sum(jnp.where(slot_perm[None, :] == frame_ids[:, None], frame_ids[None, :], 0), axis=1)
    place = frame_ids // 8
    owner = (flip(yl, place % 2) * 4 + (x + place // 2) % 4) * 2 + flip(c, place // 8)
    frame = inverse[owner * 8 + frame_ids % 8]
    te = frame % 8
    table = ((te // 2 - z + 4) % 4 * 2 + flip(te % 2, yh)) * 16 + frame // 8
    table = jnp.where(frame < clip_frames[0], table, -1).astype(jnp.int32)

    place = jnp.stack([shard_place(k) for k in range(16)]).astype(jnp.int32)

    t = tokens.reshape(8, 16, 4, 2, 200).transpose(3, 0, 2, 1, 4).reshape(2, 512, 200)
    uw, dw = fc_up, fc_down

    ua = go(uw, XBOTH)
    uo, do, uw, dw, t, place, norm_gain = phase(
        go(uw, CORE), go(dw, CORE), uw, dw, t, place, vit_gain.reshape(16, 1, 200)
    )
    p, t_zm, t_zp, ua, uao, uw, dw, do, t = phase(
        go(t, YHI), go(t, ZP), go(t, ZM), ua, go(uo, XBOTH), uw, dw, do, t
    )
    uv, p_zm, p_zp, ue, da, t_zm, uao, ua, dw, do = phase(
        go(uw, YLO), go(p, ZP), go(p, ZM), go(ua, XBOTH), go(dw, XBOTH), t_zm, uao, ua, dw, do
    )
    ub, uf = go(uv, XBOTH), go(ue, YLO)
    uvo, ua2, uao2, ue2, ua, uao, ue, t_zm, p_zp = phase(
        go(uv, CORE), go(ua, CORE), go(uao, CORE), go(ue, CORE), ua, uao, ue, t_zm, p_zp
    )
    ub, ubo, uf, t_z2, p_z2, uao, ua, ue, do, da, dw = phase(
        ub, go(uvo, XBOTH), uf, go(t_zm, ZP), go(p_zp, ZM), uao, ua, ue, do, da, dw
    )
    ub2, ubo2, uf2 = go(ub, CORE), go(ubo, CORE), go(uf, CORE)
    w_up = [uw, uo, uv, uvo, ua, ua2, uao, uao2, ue, ue2, ub, ub2, ubo, ubo2, uf, uf2]
    dao, de, dv, da, hidden, res = phase(
        go(do, XBOTH),
        go(da, XBOTH),
        go(dw, YLO),
        da,
        *up(place, [t, p, t_zp, p_zp, t_z2, p_z2, t_zm, p_zm], norm_gain, w_up),
    )
    db, df = go(dv, XBOTH), go(de, YLO)
    dvo, da2, dao2, de2, da, dao, de, hidden = phase(
        go(dv, CORE), go(da, CORE), go(dao, CORE), go(de, CORE), da, dao, de, hidden
    )
    early = down(hidden, [dw, do, dv, dvo, da, da2, dao, dao2, de, de2]).reshape(4, 128, 2000)
    db, dbo, df, up_e, down_e, hidden = phase(db, go(dvo, XBOTH), df, *ring_first(early, ZP, ZM), hidden)
    db2, dbo2, df2 = go(db, CORE), go(dbo, CORE), go(df, CORE)
    up_e, down_e = ring_second(early, up_e, down_e, ZP, ZM)
    late = down(hidden, [db, db2, dbo, dbo2, df, df2]).reshape(4, 128, 1200)
    up_e, down_e = phase(up_e, down_e)
    both_e = ring_last(early, up_e, down_e)
    other_e = go(both_e[64:].astype(BF), YHI)
    both_l = ring_sum(late, ZP, ZM)
    other_l = go(both_l[64:].astype(BF), YHI)
    parts = [both_e[:64] + other_e.astype(F32), both_l[:64] + other_l.astype(F32)]
    shuffled = layer_norm(
        parts,
        res,
        layer_scale.reshape(16, 1, 200),
        proj_gain.reshape(4, 16, 1, 200),
        proj_bias.reshape(4, 16, 1, 200),
    )
    spread = lax.all_to_all(shuffled, "dp", split_axis=0, concat_axis=0, tiled=True)
    terms = [
        jnp.dot(b.reshape(-1, 800), proj_in, preferred_element_type=F32).astype(BF).reshape(-1, 16, 1024)
        for b in gather_tensor(spread)
    ]
    ours, theirs = phase(arrange(table[:64], terms), go(arrange(table[64:], terms), CORE))
    both = add(ours, theirs).astype(BF)
    pair = ring_sum(both.reshape(4, 256, 1024), XP, XM)
    pre = pair[:128] + go(pair[128:].astype(BF), YLO).astype(F32)

    (act,) = phase(gelu(pre).astype(BF))
    terms = [None] * 4
    for dz in (2, 1, 3, 0):
        if dz == 1:
            terms[2], act = phase(terms[2], act)
        weight = lax.dynamic_slice_in_dim(proj_out, (z + dz) % 4 * 2048, 2048, 1)
        term = jnp.dot(act, weight, preferred_element_type=F32).astype(BF)
        halves = [lax.dynamic_slice_in_dim(term, flip(yh, d) * 1024, 1024, 1) for d in range(2)]
        terms[dz] = jnp.concatenate(halves, axis=0)
    pair = ring_sum(terms, ZP, ZM)
    return (pair[:128] + go(pair[128:].astype(BF), YHI).astype(F32)).astype(BF)


def solution(mesh):
    return jax.shard_map(
        shards,
        mesh=mesh,
        in_specs=(
            P("dp", "tensor"),
            P(),
            P("dp", "tensor"),
            P("dp", "tensor"),
            P(),
            P(),
            P(),
            P("dp", "tensor"),
            P("tensor", None),
            P(),
            P(),
        ),
        out_specs=P("dp", "tensor"),
        check_vma=False,
    )
```

```python
import jax
import jax.numpy as jnp
from jax import lax
from jax.experimental import pallas as pl
from jax.experimental.pallas import tpu as pltpu
from jax.sharding import PartitionSpec as P

AXES = ("dp", "tensor")
BF = jnp.bfloat16
F32 = jnp.float32


def hop(move):
    pairs = []
    for yl in range(2):
        for x in range(4):
            for c in range(2):
                for z in range(4):
                    for yh in range(2):
                        x2, yl2, c2, z2, yh2 = move(x, yl, c, z, yh)
                        src = ((yl * 4 + x) * 2 + c) * 8 + z * 2 + yh
                        dst = ((yl2 * 4 + x2 % 4) * 2 + c2) * 8 + (z2 % 4) * 2 + yh2
                        pairs.append((src, dst))
    return pairs


CORE = hop(lambda x, yl, c, z, yh: (x, yl, 1 - c, z, yh))
YLO = hop(lambda x, yl, c, z, yh: (x, 1 - yl, c, z, yh))
YHI = hop(lambda x, yl, c, z, yh: (x, yl, c, z, 1 - yh))
XP = hop(lambda x, yl, c, z, yh: (x + 1, yl, c, z, yh))
XM = hop(lambda x, yl, c, z, yh: (x + 3, yl, c, z, yh))
ZP = hop(lambda x, yl, c, z, yh: (x, yl, c, z + 1, yh))
ZM = hop(lambda x, yl, c, z, yh: (x, yl, c, z + 3, yh))
XBOTH = hop(lambda x, yl, c, z, yh: (x + 1 + 2 * c, yl, c, z, yh))
ZBOTH = hop(lambda x, yl, c, z, yh: (x, yl, c, z + 1 + 2 * c, yh))


def go(a, pairs):
    return lax.ppermute(a, AXES, pairs)


def flip(a, d):
    return a + d - 2 * a * d


def coords():
    dp = lax.axis_index("dp")
    te = lax.axis_index("tensor")
    return (dp // 2) % 4, dp // 8, dp % 2, te // 2, te % 2


SHARDS = (
    (0, 0, 0),
    (0, 0, 1),
    (0, 1, 0),
    (0, 1, 1),
    (1, 0, 0),
    (-1, 0, 1),
    (1, 0, 1),
    (-1, 0, 0),
    (2, 0, 0),
    (2, 0, 1),
    (1, 1, 0),
    (-1, 1, 1),
    (1, 1, 1),
    (-1, 1, 0),
    (2, 1, 0),
    (2, 1, 1),
)
FIRST = 10


def shard_place(k):
    x, yl, c, _, _ = coords()
    step, dy, dc = SHARDS[k]
    if step == 2:
        dx = 2
    else:
        dx = step * (2 * c - 1) + 4
    return (flip(yl, dy) * 4 + (x + dx) % 4) * 2 + flip(c, dc)


def phase(*values):
    return lax.optimization_barrier(values)


def gather_tensor(a):
    half = a.shape[0] // 2
    zm_o, zp_o = go(a, ZP), go(a, ZM)
    z2_o = jnp.concatenate([go(zm_o[:half], ZP), go(zp_o[half:], ZM)], axis=0)
    _, _, p = phase(zm_o, zp_o, go(a, YHI))
    zm_p, zp_p = go(p, ZP), go(p, ZM)
    z2_p = go(z2_o, YHI)
    return [a, p, zp_o, zp_p, z2_o, z2_p, zm_o, zm_p]


def add(a, b):
    return a.astype(F32) + b.astype(F32)


def ring_first(u, plus, minus):
    half = u[2].shape[0] // 2
    return go(u[2][:half], plus), go(u[2][half:], minus)


def ring_second(u, up, down, plus, minus):
    half = u[2].shape[0] // 2
    first = jnp.concatenate([add(u[1][:half], up).astype(BF), u[1][half:]], axis=0)
    third = jnp.concatenate([u[3][:half], add(u[3][half:], down).astype(BF)], axis=0)
    first, third = phase(first, third)
    return go(first, plus), go(third, minus)


def ring_last(u, up, down):
    return u[0].astype(F32) + up.astype(F32) + down.astype(F32)


def ring_sum(u, plus, minus):
    up, down = phase(*ring_first(u, plus, minus))
    up, down = phase(*ring_second(u, up, down, plus, minus))
    return ring_last(u, up, down)


def gelu(v):
    return 0.5 * v * (1.0 + lax.erf(v * 0.7071067811865476))


ANY = pl.BlockSpec(memory_space=pl.ANY)
VMEM = pl.BlockSpec(memory_space=pltpu.VMEM)
SMEM = pl.BlockSpec(memory_space=pltpu.SMEM)


def frame_of(r):
    _, _, _, z, yh = coords()
    return ((z + r // 2) % 4) * 2 + flip(yh, r % 2)


def up_body(place, *refs):
    blocks, gain, shards = refs[:8], refs[8], refs[9:25]
    out, res, xs, scaled, held, squares, xsems, sems = refs[25:]
    xcopies = [
        pltpu.make_async_copy(blocks[i], xs.at[pl.ds(frame_of(i) * 2, 2)], xsems.at[i]) for i in range(8)
    ]
    copies = [pltpu.make_async_copy(shards[k], held.at[k], sems.at[k]) for k in range(16)]
    for cp in xcopies + copies:
        cp.start()
    squares[...] = jnp.zeros_like(squares)
    for cp in xcopies:
        cp.wait()

    def shard(k, _):
        p = place[k]
        for r in range(8):
            v = xs[p, pl.ds(pl.multiple_of(frame_of(r) * 64, 64), 64), :].astype(F32)
            squares[r * 64 : r * 64 + 64, :] += v * v
            scaled[k, r * 64 : r * 64 + 64, :] = (v * gain[p]).astype(BF)
        return 0

    lax.fori_loop(0, 16, shard, 0)
    scale = lax.rsqrt(jnp.sum(squares[...], axis=1, keepdims=True) * (1.0 / 3200.0) + 1e-06)
    own = pl.ds(pl.multiple_of(frame_of(0) * 64, 64), 64)
    for p in range(16):
        res[p] = xs[p, own, :]
    for cp in copies:
        cp.wait()
    for start in range(0, 1600, 256):
        end = min(start + 256, 1600)
        act = jnp.dot(scaled[0], held[0, :, start:end], preferred_element_type=F32)
        for k in range(1, 16):
            act += jnp.dot(scaled[k], held[k, :, start:end], preferred_element_type=F32)
        out[:, start:end] = gelu(act * scale).astype(BF)


def up(place, blocks, gain, shards):
    return pl.pallas_call(
        up_body,
        out_shape=(jax.ShapeDtypeStruct((512, 1600), BF), jax.ShapeDtypeStruct((16, 64, 200), BF)),
        in_specs=[SMEM] + [ANY] * 8 + [VMEM] + [ANY] * 16,
        out_specs=(VMEM, VMEM),
        scratch_shapes=[
            pltpu.VMEM((16, 512, 200), BF),
            pltpu.VMEM((16, 512, 200), BF),
            pltpu.VMEM((16, 200, 1600), BF),
            pltpu.VMEM((512, 200), F32),
            pltpu.SemaphoreType.DMA((8,)),
            pltpu.SemaphoreType.DMA((16,)),
        ],
        compiler_params=pltpu.CompilerParams(vmem_limit_bytes=28 << 20),
        cost_estimate=pl.CostEstimate(flops=1 << 20, bytes_accessed=1 << 16, transcendentals=0),
        name="up",
    )(place, *blocks, gain, *shards)


def down(hidden, shards):
    rows = jnp.concatenate(shards, axis=0)
    return lax.dot_general(hidden, rows, (((1,), (1,)), ((), ())), preferred_element_type=F32).astype(BF)


def ln_body(br0, br1, res, ls, gain, bias, out, held):
    total = jnp.zeros((64, 1), F32)
    for k in range(16):
        if k < FIRST:
            b = br0[:, k * 200 : k * 200 + 200]
        else:
            b = br1[:, (k - FIRST) * 200 : (k - FIRST) * 200 + 200]
        p = shard_place(k)
        v = (res[p].astype(F32) + ls[p] * b).astype(BF).astype(F32)
        held[p] = v
        total += jnp.sum(v, axis=1, keepdims=True)
    mean = (total[0:16] + total[16:32] + total[32:48] + total[48:64]) * (1.0 / 12800.0)
    mean = jnp.concatenate([mean] * 4, axis=0)
    total = jnp.zeros((64, 1), F32)
    for p in range(16):
        v = held[p] - mean
        total += jnp.sum(v * v, axis=1, keepdims=True)
    var = (total[0:16] + total[16:32] + total[32:48] + total[48:64]) * (1.0 / 12800.0)
    inv = jnp.concatenate([lax.rsqrt(var + 1e-05)] * 4, axis=0)
    for p in range(16):
        v = (held[p] - mean) * inv
        for q in range(4):
            piece = v[q * 16 : q * 16 + 16] * gain[q, p] + bias[q, p]
            out[q * 4 + p // 4, :, (p % 4) * 200 : (p % 4) * 200 + 200] = piece.astype(BF)


def layer_norm(parts, res, ls, gain, bias):
    return pl.pallas_call(
        ln_body,
        out_shape=jax.ShapeDtypeStruct((16, 16, 800), BF),
        in_specs=[VMEM] * 6,
        out_specs=VMEM,
        scratch_shapes=[pltpu.VMEM((16, 64, 200), F32)],
        compiler_params=pltpu.CompilerParams(vmem_limit_bytes=8 << 20),
        cost_estimate=pl.CostEstimate(flops=1 << 20, bytes_accessed=1 << 16, transcendentals=0),
        name="layer_norm",
    )(*parts, res, ls, gain, bias)


def arrange_body(table, *refs):
    blocks, out, held, sems = refs[:8], refs[8], refs[9], refs[10]
    copies = [pltpu.make_async_copy(blocks[i], held.at[pl.ds(i * 16, 16)], sems.at[i]) for i in range(8)]
    for cp in copies:
        cp.start()
    for cp in copies:
        cp.wait()

    def tile(m, _):
        for s in range(8):
            at = table[m * 8 + s]
            v = held[jnp.maximum(at, 0)]
            rows = pl.ds(pl.multiple_of(m * 128 + s * 16, 16), 16)
            out[rows, :] = jnp.where(at >= 0, v, jnp.zeros_like(v))
        return 0

    lax.fori_loop(0, 16, tile, 0)


def arrange(table, blocks):
    return pl.pallas_call(
        arrange_body,
        out_shape=jax.ShapeDtypeStruct((2048, 800), BF),
        in_specs=[SMEM] + [ANY] * 8,
        out_specs=VMEM,
        scratch_shapes=[pltpu.VMEM((128, 16, 800), BF), pltpu.SemaphoreType.DMA((8,))],
        compiler_params=pltpu.CompilerParams(vmem_limit_bytes=10 << 20),
        cost_estimate=pl.CostEstimate(flops=1 << 20, bytes_accessed=1 << 16, transcendentals=0),
        name="arrange",
    )(table, *blocks)


def shards(
    tokens,
    vit_gain,
    fc_up,
    fc_down,
    layer_scale,
    proj_gain,
    proj_bias,
    proj_in,
    proj_out,
    clip_frames,
    slot_perm,
):
    x, yl, c, z, yh = coords()

    frame_ids = jnp.arange(128, dtype=jnp.int32)
    inverse = jnp.sum(jnp.where(slot_perm[None, :] == frame_ids[:, None], frame_ids[None, :], 0), axis=1)
    place = frame_ids // 8
    owner = (flip(yl, place % 2) * 4 + (x + place // 2) % 4) * 2 + flip(c, place // 8)
    frame = inverse[owner * 8 + frame_ids % 8]
    te = frame % 8
    table = ((te // 2 - z + 4) % 4 * 2 + flip(te % 2, yh)) * 16 + frame // 8
    table = jnp.where(frame < clip_frames[0], table, -1).astype(jnp.int32)

    place = jnp.stack([shard_place(k) for k in range(16)]).astype(jnp.int32)

    t = tokens.reshape(8, 16, 4, 2, 200).transpose(3, 0, 2, 1, 4).reshape(2, 512, 200)
    uw, dw = fc_up, fc_down

    ua = go(uw, XBOTH)
    uo, do, uw, dw, t, place, norm_gain = phase(
        go(uw, CORE), go(dw, CORE), uw, dw, t, place, vit_gain.reshape(16, 1, 200)
    )
    p, t_zm, t_zp, ua, uao, uw, dw, do, t = phase(
        go(t, YHI), go(t, ZP), go(t, ZM), ua, go(uo, XBOTH), uw, dw, do, t
    )
    uv, p_zm, p_zp, ue, da, t_zm, uao, ua, dw, do = phase(
        go(uw, YLO), go(p, ZP), go(p, ZM), go(ua, XBOTH), go(dw, XBOTH), t_zm, uao, ua, dw, do
    )
    ub, uf = go(uv, XBOTH), go(ue, YLO)
    uvo, ua2, uao2, ue2, ua, uao, ue, t_zm, p_zp = phase(
        go(uv, CORE), go(ua, CORE), go(uao, CORE), go(ue, CORE), ua, uao, ue, t_zm, p_zp
    )
    ub, ubo, uf, t_z2, p_z2, uao, ua, ue, do, da, dw = phase(
        ub, go(uvo, XBOTH), uf, go(t_zm, ZP), go(p_zp, ZM), uao, ua, ue, do, da, dw
    )
    ub2, ubo2, uf2 = go(ub, CORE), go(ubo, CORE), go(uf, CORE)
    w_up = [uw, uo, uv, uvo, ua, ua2, uao, uao2, ue, ue2, ub, ub2, ubo, ubo2, uf, uf2]
    dao, de, dv, da, hidden, res = phase(
        go(do, XBOTH),
        go(da, XBOTH),
        go(dw, YLO),
        da,
        *up(place, [t, p, t_zp, p_zp, t_z2, p_z2, t_zm, p_zm], norm_gain, w_up),
    )
    db, df = go(dv, XBOTH), go(de, YLO)
    dvo, da2, dao2, de2, da, dao, de, hidden = phase(
        go(dv, CORE), go(da, CORE), go(dao, CORE), go(de, CORE), da, dao, de, hidden
    )
    early = down(hidden, [dw, do, dv, dvo, da, da2, dao, dao2, de, de2]).reshape(4, 128, 2000)
    db, dbo, df, up_e, down_e, hidden = phase(db, go(dvo, XBOTH), df, *ring_first(early, ZP, ZM), hidden)
    db2, dbo2, df2 = go(db, CORE), go(dbo, CORE), go(df, CORE)
    up_e, down_e = ring_second(early, up_e, down_e, ZP, ZM)
    late = down(hidden, [db, db2, dbo, dbo2, df, df2]).reshape(4, 128, 1200)
    up_e, down_e = phase(up_e, down_e)
    both_e = ring_last(early, up_e, down_e)
    other_e = go(both_e[64:].astype(BF), YHI)
    both_l = ring_sum(late, ZP, ZM)
    other_l = go(both_l[64:].astype(BF), YHI)
    parts = [both_e[:64] + other_e.astype(F32), both_l[:64] + other_l.astype(F32)]
    shuffled = layer_norm(
        parts,
        res,
        layer_scale.reshape(16, 1, 200),
        proj_gain.reshape(4, 16, 1, 200),
        proj_bias.reshape(4, 16, 1, 200),
    )
    spread = lax.all_to_all(shuffled, "dp", split_axis=0, concat_axis=0, tiled=True)
    rows = arrange(table, gather_tensor(spread))
    theirs = jnp.dot(rows[1024:], proj_in, preferred_element_type=F32).astype(BF)
    ours, theirs = phase(jnp.dot(rows[:1024], proj_in, preferred_element_type=F32).astype(BF), go(theirs, CORE))
    both = add(ours, theirs).astype(BF)
    pair = ring_sum(both.reshape(4, 256, 1024), XP, XM)
    pre = pair[:128] + go(pair[128:].astype(BF), YLO).astype(F32)

    (act,) = phase(gelu(pre).astype(BF))
    terms = [None] * 4
    for dz in (2, 1, 3, 0):
        if dz == 1:
            terms[2], act = phase(terms[2], act)
        weight = lax.dynamic_slice_in_dim(proj_out, (z + dz) % 4 * 2048, 2048, 1)
        term = jnp.dot(act, weight, preferred_element_type=F32).astype(BF)
        halves = [lax.dynamic_slice_in_dim(term, flip(yh, d) * 1024, 1024, 1) for d in range(2)]
        terms[dz] = jnp.concatenate(halves, axis=0)
    up_t, down_t = phase(*ring_first(terms, ZP, ZM))
    first = jnp.concatenate([add(terms[1][:128], up_t).astype(BF), terms[1][128:]], axis=0)
    third = jnp.concatenate([terms[3][:128], add(terms[3][128:], down_t).astype(BF)], axis=0)
    pair = ring_last(terms, *phase(go(first, ZP), go(third, ZM)))
    return (pair[:128] + go(pair[128:].astype(BF), YHI).astype(F32)).astype(BF)


def solution(mesh):
    return jax.shard_map(
        shards,
        mesh=mesh,
        in_specs=(
            P("dp", "tensor"),
            P(),
            P("dp", "tensor"),
            P("dp", "tensor"),
            P(),
            P(),
            P(),
            P("dp", "tensor"),
            P("tensor", None),
            P(),
            P(),
        ),
        out_specs=P("dp", "tensor"),
        check_vma=False,
    )
```
